32 devices in a mesh: date: 4 (over y, core), tile: 8 (over z, x).
Axes of the slice: x: 2, y: 2, z: 4, core: 2. Of those that a mesh axis runs over, the one named last changes fastest.
Arguments:
- radar_echoes: bfloat16 [512, 16, 16, 2, 256], P('tile', None, 'date')
- destination_panel: int32 [512, 1], P('tile'), may hold values from 0 to 7; in each aligned block of 64 rows (0 to 63, 64 to 127, ...) at most 12 rows name the same one
- panel_line_shift: int32 [512], P('tile'), may hold values from 0 to 240
- epoch_couples: int32 [32, 2], replicated, may hold values from 0 to 15, as said below
Outputs:
- coherence: float32 [2048, 32, 256], P('tile', 'date')
The draws below stay inside these ranges and needn't reach their ends.
Inputs may be any that keep to these rules, and one draw needn't show every extreme that they name: `destination_panel`: of the blocks held by one index of tile, at most 12 land on the same tile; some index reaches it. `epoch_couples`: each row names an earlier date and a later one, 1 to 3 dates apart.
All inputs are finite; a program needn't handle non-finite values.
Results may differ from the reference program's by a relative error of at most 0.00079.
Values may be sent and summed in bfloat16 or wider, within the bound.
No kernel may reach another device: no remote copies, remote signals or barrier semaphores. Data moves between devices by JAX's collectives and lax.ppermute only.
A program may use at most 64 MiB of HBM per device.

```python
import math
import jax
import jax.numpy as jnp
import numpy as np
from jax import lax

TC = 256
BR = 16
TR = 256
BLK_DEV = 64
CAP = 12
SRC_BLOCKS = 512
DATES = 16
PAIRS = 32
N_TILE = 8


def draw_radar_echoes(key, part):
    common = jax.random.normal(jax.random.fold_in(key, 11), (SRC_BLOCKS, BR, 1, 2, TC), jnp.float32)
    own = jax.random.normal(jax.random.fold_in(key, 12), (SRC_BLOCKS, BR, DATES, 2, TC), jnp.float32)
    rho = jax.random.uniform(jax.random.fold_in(key, 13), (SRC_BLOCKS, 1, DATES, 1, 1), jnp.float32, 0.2, 0.95)
    amplitude = jax.random.uniform(jax.random.fold_in(key, 14), (SRC_BLOCKS, BR, 1, 1, TC), jnp.float32, 0.5, 1.5)
    value = amplitude * (rho * common + jnp.sqrt(1.0 - rho * rho) * own)
    value = jnp.clip(value, -40.0, 40.0)
    return value.astype(jnp.bfloat16)


def draw_epoch_couples(key, part):
    spacing = jax.random.randint(jax.random.fold_in(key, 21), (PAIRS,), 1, 4)
    earlier = jax.random.randint(jax.random.fold_in(key, 22), (PAIRS,), 0, DATES - 3)
    places = jnp.arange(PAIRS)
    earlier = jnp.where(places == 0, DATES - 1 - spacing, earlier)
    earlier = jnp.where(places == 1, 0, earlier)
    return jnp.stack([earlier, earlier + spacing], axis=1).astype(jnp.int32)


def place_ends(values, own_key, low, top_value):
    index_at = [jax.random.randint(jax.random.fold_in(own_key, axis), (), 0, length) for axis, length in enumerate(values.shape)]
    widest = values.shape.index(max(values.shape))
    neighbour = index_at[:widest] + [(index_at[widest] + 1) % values.shape[widest]] + index_at[widest + 1:]
    return values.at[tuple(index_at)].set(low).at[tuple(neighbour)].set(top_value)


def assign_block(rng, own, number, rows, number_of, top, bound, lean):
    order = jax.random.permutation(rng, number_of)
    packed, ordinary = shares(number_of, rows * top, bound, lean, True), shares(number_of, rows * top, bound, lean, False)
    places = jnp.arange(number_of)

    def named(lengths, turn):
        used = int((lengths > 0).sum())
        fixed = max(1, used // 4)
        moved = fixed + (places - fixed + turn * (used - fixed)) % max(1, number_of - fixed)
        return jnp.zeros((number_of,), jnp.int32).at[order[jnp.where(places < fixed, places, moved)]].set(jnp.asarray(lengths, jnp.int32))

    lengths = jnp.where(number % 4 == 0, named(packed, number // 4), named(ordinary, number - number // 4 - 1))
    mixed = jax.random.permutation(jax.random.fold_in(own, 3), number_of)
    giver, receiver = mixed[0:number_of // 2 * 2:2], mixed[1:number_of // 2 * 2:2]
    room = jnp.minimum(lengths[giver] - 1, bound - lengths[receiver]) // 2
    room = jnp.where((giver == order[0]) | (receiver == order[0]) | (lengths[receiver] == 0), 0, jnp.maximum(room, 0))
    moved = jax.random.randint(jax.random.fold_in(own, 4), (number_of // 2,), 0, 1 << 20) % (room + 1)
    lengths = lengths.at[giver].add(-moved).at[receiver].add(moved)
    items = jnp.searchsorted(jnp.cumsum(lengths), jnp.arange(rows * top), side="right").astype(jnp.int32)
    table = items.reshape(top, rows).T
    table = table[jax.random.permutation(jax.random.fold_in(own, 1), rows)]
    turn = jax.random.randint(jax.random.fold_in(own, 2), (rows, 1), 0, top)
    return jnp.take_along_axis(table, (jnp.arange(top)[None, :] + turn) % top, axis=1)


def shares(count, total, reach, lean, full):
    weights = [(1 << 20) // math.isqrt(standing ** lean) + 1 for standing in range(1, count + 1)]
    largest = reach if full else min(reach, max(-(-total // count), total * weights[0] // sum(weights)))
    least = 1 if total - largest >= count - 1 else 0
    holding, spare = [largest] + [least] * (count - 1), total - largest - least * (count - 1)
    while spare > 0:
        movable = [i for i in range(1, count) if holding[i] < largest] or [i for i in range(1, count) if holding[i] < reach]
        mass, left = sum([weights[i] for i in movable]), spare
        for i in movable:
            extra = min(reach - holding[i], max(1, left * weights[i] // mass), spare)
            holding[i] = holding[i] + extra
            spare = spare - extra
    return np.array(holding)


def setup_inputs(seed: int = 0) -> dict:
    streams_of = jax.random.split(jax.random.key(seed), 5)
    radar_echoes = draw_radar_echoes(jax.random.fold_in(streams_of[4], 71), 0)
    destination_panel_keys = jax.random.split(jax.random.fold_in(streams_of[1], 1), SRC_BLOCKS // BLK_DEV)
    destination_panel_turns = jax.random.permutation(jax.random.fold_in(streams_of[1], 3), SRC_BLOCKS // BLK_DEV)
    destination_panel = jax.vmap(lambda own, number: assign_block(jax.random.fold_in(streams_of[1], 2), own, number, BLK_DEV, N_TILE, 1, CAP, 2))(destination_panel_keys, destination_panel_turns).reshape((SRC_BLOCKS, 1))
    panel_line_shift = place_ends(jax.random.randint(streams_of[2], (SRC_BLOCKS,), 0, TR - BR + 1), jax.random.fold_in(streams_of[2], 1), 0, TR - BR).astype(jnp.int32)
    epoch_couples = draw_epoch_couples(jax.random.fold_in(streams_of[4], 71), 0)
    return {"radar_echoes": radar_echoes, "destination_panel": destination_panel, "panel_line_shift": panel_line_shift, "epoch_couples": epoch_couples}


def window_sum(field, rows):
    total = field[0:rows]
    for row_lag in range(1, 7):
        total = total + field[row_lag:row_lag + rows]
    cols = total.shape[-1]
    padded = jnp.pad(total, ((0, 0), (0, 0), (7, 7)))
    result = padded[..., 0:cols]
    for column_lag in range(1, 15):
        result = result + padded[..., column_lag:column_lag + cols]
    return result

def coherence_of(first, second, rows):
    first = first.astype(jnp.float32)
    second = second.astype(jnp.float32)
    first_re, first_im = (first[:, :, 0], first[:, :, 1])
    second_re, second_im = (second[:, :, 0], second[:, :, 1])
    cross_re = first_re * second_re + first_im * second_im
    cross_im = first_im * second_re - first_re * second_im
    power_a = first_re * first_re + first_im * first_im
    power_e = second_re * second_re + second_im * second_im
    box_re = window_sum(cross_re, rows)
    box_im = window_sum(cross_im, rows)
    box_a = window_sum(power_a, rows)
    box_e = window_sum(power_e, rows)
    return jnp.sqrt(box_re * box_re + box_im * box_im) / jnp.sqrt(jnp.maximum(box_a * box_e, 1.0))

def reference(radar_echoes, destination_panel, panel_line_shift, epoch_couples):
    opening_lines = (destination_panel[:, 0] * TR + panel_line_shift).astype(jnp.int32)
    panel_raster = jnp.zeros((N_TILE * TR, DATES, 2, TC), jnp.float32)

    def deposit_patch(carry, item):
        block, start = item
        current = lax.dynamic_slice_in_dim(carry, start, BR, 0)
        return (lax.dynamic_update_slice_in_dim(carry, current + block.astype(jnp.float32), start, 0), None)
    panel_raster, ignored_value = lax.scan(deposit_patch, panel_raster, (radar_echoes, opening_lines))
    panel_raster = panel_raster.astype(jnp.bfloat16).reshape(N_TILE, TR, DATES, 2, TC)
    panel_raster = jnp.transpose(panel_raster, (1, 0, 2, 3, 4))
    panel_raster = jnp.pad(panel_raster, ((3, 3), (0, 0), (0, 0), (0, 0), (0, 0)))

    def one_pair(pair_row):
        first = lax.dynamic_index_in_dim(panel_raster, pair_row[0], axis=2, keepdims=False)
        second = lax.dynamic_index_in_dim(panel_raster, pair_row[1], axis=2, keepdims=False)
        return coherence_of(first, second, TR)
    result = lax.map(one_pair, epoch_couples)
    result = jnp.transpose(result, (2, 1, 0, 3))
    return result.reshape(N_TILE * TR, PAIRS, TC)
```

```python
import functools

import jax
import jax.numpy as jnp
from jax import lax
from jax.experimental import pallas as pl
from jax.experimental.pallas import tpu as pltpu
from jax.sharding import PartitionSpec as P

TR = 256
LANES = 128
ROW_SPACE = 1 << 16
VMEM_BYTES = 48 * 1024 * 1024


def flip_pairs(axis, mask):
    return [(i, i ^ mask) for i in range(lax.axis_size(axis))]


def swap(value, axis, mask):
    return lax.ppermute(value, axis, flip_pairs(axis, mask))


def pick_kernel(code_ref, blocks_ref, out_ref, meta_ref):
    def body(b, count):
        code = code_ref[b]
        crosses = (code // ROW_SPACE) % 2

        @pl.when(crosses == 1)
        def _():
            out_ref[count] = blocks_ref[b, :, 0]
            meta_ref[count] = code

        return count + crosses

    count = lax.fori_loop(0, blocks_ref.shape[0], body, jnp.int32(0))
    meta_ref[meta_ref.shape[0] - 1] = count


def pick(code, view, date, slots):
    blocks, height, _, parts, lanes = view.shape
    return pl.pallas_call(
        pick_kernel,
        grid=(1,),
        in_specs=[
            pl.BlockSpec(memory_space=pltpu.SMEM),
            pl.BlockSpec((blocks, height, 1, parts, lanes), lambda i: (0, 0, date, 0, 0)),
        ],
        out_specs=[
            pl.BlockSpec((slots, height, parts, lanes), lambda i: (0, 0, 0, 0)),
            pl.BlockSpec(memory_space=pltpu.SMEM),
        ],
        out_shape=[
            jax.ShapeDtypeStruct((slots, height, parts, lanes), view.dtype),
            jax.ShapeDtypeStruct((slots + 1,), jnp.int32),
        ],
        compiler_params=pltpu.CompilerParams(vmem_limit_bytes=VMEM_BYTES),
    )(code, view)


def deposit_kernel(code_ref, meta_ref, blocks_ref, got_ref, send_ref, keep_ref, acc_ref):
    height = blocks_ref.shape[1]
    tiles, rows, parts, lanes = acc_ref.shape

    def clear(t, _):
        acc_ref[t] = jnp.zeros((rows, parts, lanes), jnp.float32)
        return 0

    lax.fori_loop(0, tiles, clear, 0)

    def add(code, block):
        tile = code // (2 * ROW_SPACE)
        row = code % ROW_SPACE
        span = pl.ds(row, height)
        acc_ref[tile, span] = acc_ref[tile, span] + block.astype(jnp.float32)

    def own(b, _):
        code = code_ref[b]

        @pl.when((code // ROW_SPACE) % 2 == 0)
        def _():
            add(code, blocks_ref[b, :, 0])

        return 0

    lax.fori_loop(0, blocks_ref.shape[0], own, 0)

    def received(k, _):
        add(meta_ref[k], got_ref[k])
        return 0

    lax.fori_loop(0, meta_ref[meta_ref.shape[0] - 1], received, 0)

    flat = acc_ref.reshape(tiles, rows * parts, lanes)

    def hand_over(i, _):
        for part in range(parts):
            keep_ref[i, part] = flat[2 * i, pl.ds(part, rows, stride=parts)]
            send_ref[i, part] = flat[2 * i + 1, pl.ds(part, rows, stride=parts)].astype(send_ref.dtype)
        return 0

    lax.fori_loop(0, tiles // 2, hand_over, 0)


def deposit(code, meta, view, got, date, tiles):
    blocks, height, _, parts, lanes = view.shape
    dense = (tiles // 2, parts, TR, lanes)
    return pl.pallas_call(
        deposit_kernel,
        grid=(1,),
        in_specs=[
            pl.BlockSpec(memory_space=pltpu.SMEM),
            pl.BlockSpec(memory_space=pltpu.SMEM),
            pl.BlockSpec((blocks, height, 1, parts, lanes), lambda i: (0, 0, date, 0, 0)),
            pl.BlockSpec(got.shape, lambda i: (0, 0, 0, 0)),
        ],
        out_specs=[
            pl.BlockSpec(dense, lambda i: (0, 0, 0, 0)),
            pl.BlockSpec(dense, lambda i: (0, 0, 0, 0)),
        ],
        out_shape=[
            jax.ShapeDtypeStruct(dense, view.dtype),
            jax.ShapeDtypeStruct(dense, jnp.float32),
        ],
        scratch_shapes=[pltpu.VMEM((tiles, TR, parts, lanes), jnp.float32)],
        compiler_params=pltpu.CompilerParams(vmem_limit_bytes=VMEM_BYTES),
    )(code, meta, view, got)


def split(value):
    high = value.astype(jnp.bfloat16)
    low = (value - high.astype(jnp.float32)).astype(jnp.bfloat16)
    return high, low


def band(size, reach):
    row = lax.broadcasted_iota(jnp.int32, (size, size), 0)
    col = lax.broadcasted_iota(jnp.int32, (size, size), 1)
    return (jnp.abs(row - col) <= reach).astype(jnp.bfloat16)


def coherence_kernel(pairs_ref, *refs):
    *field_refs, out_ref, held, done, sems, out_sems = refs
    copies = [
        pltpu.make_async_copy(ref, held.at[k], sems.at[k]) for k, ref in enumerate(field_refs)
    ]
    for copy in copies:
        copy.start()
    rows, pairs, cols = out_ref.shape
    row_band = band(rows, 3)
    col_band = band(cols, 7)
    halves = cols // held.shape[-1]
    for copy in copies:
        copy.wait()

    def box(value):
        high, low = split(value)
        wide = jnp.dot(high, col_band, preferred_element_type=jnp.float32)
        wide = wide + jnp.dot(low, col_band, preferred_element_type=jnp.float32)
        high, low = split(wide)
        total = jnp.dot(row_band, high, preferred_element_type=jnp.float32)
        return total + jnp.dot(row_band, low, preferred_element_type=jnp.float32)

    def field(index, component):
        sides = [held[index, 2 * half + component] for half in range(halves)]
        return jnp.concatenate(sides, axis=-1).astype(jnp.float32)

    for p in range(pairs):
        first, second = pairs_ref[2 * p], pairs_ref[2 * p + 1]
        u0, u1 = field(first, 0), field(first, 1)
        v0, v1 = field(second, 0), field(second, 1)
        box_re = box(u0 * v0 + u1 * v1)
        box_im = box(u1 * v0 - u0 * v1)
        box_a = box(u0 * u0 + u1 * u1)
        box_e = box(v0 * v0 + v1 * v1)
        value = jnp.sqrt(box_re * box_re + box_im * box_im) * lax.rsqrt(
            jnp.maximum(box_a * box_e, 1.0)
        )
        for half in range(halves):
            side = value[:, half * LANES : (half + 1) * LANES]
            done.at[half].reshape(rows * pairs, LANES)[pl.ds(p, rows, stride=pairs)] = side
    leaving = [
        pltpu.make_async_copy(
            done.at[half], out_ref.at[:, :, pl.ds(half * LANES, LANES)], out_sems.at[half]
        )
        for half in range(halves)
    ]
    for copy in leaving:
        copy.start()
    for copy in leaving:
        copy.wait()


def coherence(pairs, fields, out_shape):
    parts, rows, lanes = fields[0].shape
    return pl.pallas_call(
        coherence_kernel,
        in_specs=[pl.BlockSpec(memory_space=pltpu.SMEM)]
        + [pl.BlockSpec(memory_space=pl.ANY)] * len(fields),
        out_specs=pl.BlockSpec(memory_space=pl.ANY),
        out_shape=jax.ShapeDtypeStruct(out_shape, jnp.float32),
        scratch_shapes=[
            pltpu.VMEM((len(fields), parts, rows, lanes), fields[0].dtype),
            pltpu.VMEM((out_shape[2] // lanes, rows, out_shape[1], lanes), jnp.float32),
            pltpu.SemaphoreType.DMA((len(fields),)),
            pltpu.SemaphoreType.DMA((out_shape[2] // lanes,)),
        ],
        compiler_params=pltpu.CompilerParams(vmem_limit_bytes=VMEM_BYTES),
    )(pairs, *fields)


def local(radar_echoes, destination_panel, panel_line_shift, epoch_couples):
    blocks, height, dates_here, components, cols = radar_echoes.shape
    tile_count = lax.axis_size("tile")
    group_count = lax.axis_size("date")
    here = lax.axis_index("tile")
    group = lax.axis_index("date")
    capacity = max(2, blocks // tile_count + max(1, blocks // (2 * tile_count)))
    slots = min(blocks, tile_count // 2 * capacity)

    halves = cols // LANES
    view = radar_echoes.reshape(blocks, height, dates_here, components, halves, LANES)
    view = view.transpose(0, 1, 2, 4, 3, 5)
    view = view.reshape(blocks, height, dates_here, halves * components, LANES)

    relative = jnp.bitwise_xor(destination_panel[:, 0], here)
    code = relative * ROW_SPACE + panel_line_shift

    groups = {}
    meta = None
    for date in range(dates_here):
        packed, own_meta = pick(code, view, date, slots)
        if meta is None:
            meta = swap(own_meta, "tile", 1)
        got = swap(packed, "tile", 1)
        send, keep = deposit(code, meta, view, got, date, tile_count // 2)
        mask = 2
        while True:
            total = keep + swap(send, "tile", mask).astype(jnp.float32)
            if total.shape[0] == 1:
                break
            keep, send = total[0::2], total[1::2].astype(view.dtype)
            mask *= 2
        field = total[0].astype(view.dtype)
        known = {0: field}
        mask = group_count // 2
        while mask:
            known.update({g ^ mask: swap(f, "date", mask) for g, f in list(known.items())})
            mask //= 2
        for g, f in known.items():
            groups[g * dates_here + date] = f
    fields = [groups[k] for k in range(group_count * dates_here)]

    pairs_here = epoch_couples.shape[0] // group_count
    mine = lax.dynamic_slice_in_dim(epoch_couples, group * pairs_here, pairs_here, axis=0)
    place = jnp.bitwise_xor(mine // dates_here, group) * dates_here + mine % dates_here
    return coherence(place.reshape(-1), fields, (TR, pairs_here, cols))


def solution(mesh):
    in_specs = (P("tile", None, "date", None, None), P("tile", None), P("tile"), P())
    out_specs = P("tile", "date", None)
    return jax.shard_map(local, mesh=mesh, in_specs=in_specs, out_specs=out_specs, check_vma=False)
```

```python
import functools

import jax
import jax.numpy as jnp
from jax import lax
from jax.experimental import pallas as pl
from jax.experimental.pallas import tpu as pltpu
from jax.sharding import PartitionSpec as P

TR = 256
LANES = 128
SUBLANES = 8
ROW_SPACE = 1 << 16
CROSS = 1 << 24
MIB = 1024 * 1024
CHEAP = pl.CostEstimate(flops=1, bytes_accessed=1, transcendentals=0)
SMEM = pl.BlockSpec(memory_space=pltpu.SMEM)
VMEM = pl.BlockSpec(memory_space=pltpu.VMEM)
ANY = pl.BlockSpec(memory_space=pl.ANY)


def params(mib):
    return pltpu.CompilerParams(vmem_limit_bytes=mib * MIB)


def swap(value, axis, mask):
    pairs = [(i, i ^ mask) for i in range(lax.axis_size(axis))]
    return lax.ppermute(value, axis, pairs)


def block_codes(target, row, here, order):
    relative = jnp.bitwise_xor(target, here)
    first, *others = [(relative // (1 << bit)) % 2 for bit in order]
    place = sum([bit * (1 << k) for k, bit in enumerate(others)], jnp.zeros_like(relative))
    return first * CROSS + place * ROW_SPACE + row


def unpack(code):
    place = jnp.bitwise_and(lax.shift_right_logical(code, 16), CROSS // ROW_SPACE - 1)
    return lax.shift_right_logical(code, 24), place, jnp.bitwise_and(code, ROW_SPACE - 1)


def pick_kernel(code_ref, blocks_ref, *refs):
    out_ref, count_ref = refs[-2:]
    step = pl.program_id(0)
    share = blocks_ref.shape[0]

    @pl.when(step == 0)
    def _():
        count_ref[0] = 0

    def body(b, count):
        crosses = lax.shift_right_logical(code_ref[step * share + b], 24)

        @pl.when(crosses == 1)
        def _():
            out_ref[count] = blocks_ref[b, :, 0]

        return count + crosses

    count_ref[0] = lax.fori_loop(0, share, body, count_ref[0])


def pick(codes, view, date, slots, tokens):
    blocks, height, _, parts, lanes = view.shape
    steps = PICK_STEPS if blocks % PICK_STEPS == 0 else 1
    return pl.pallas_call(
        pick_kernel,
        grid=(steps,),
        in_specs=[
            SMEM,
            pl.BlockSpec((blocks // steps, height, 1, parts, lanes), lambda i: (i, 0, date, 0, 0)),
        ]
        + [ANY if token.ndim > 1 else SMEM for token in tokens],
        out_specs=VMEM,
        out_shape=jax.ShapeDtypeStruct((slots, height, parts, lanes), view.dtype),
        scratch_shapes=[pltpu.SMEM((1,), jnp.int32)],
        cost_estimate=CHEAP,
        compiler_params=params(PICK_MIB),
        name="pick",
    )(codes, view, *tokens)


def deposit_kernel(
    date, code_ref, partner_ref, view_ref, got_ref, token_ref, far_ref, near_ref, keep_ref, acc_ref, own_ref, sem
):
    del token_ref
    count, height = own_ref.shape[:2]
    tiles, rows, parts, lanes = acc_ref.shape
    fetch = pltpu.make_async_copy(view_ref.at[:, :, date], own_ref, sem)
    fetch.start()
    flat = acc_ref.reshape(tiles, rows * parts, lanes)

    def clear(t, _):
        flat[t] = jnp.zeros((rows * parts, lanes), jnp.float32)
        return 0

    lax.fori_loop(0, tiles, clear, 0)

    def add(tile, row, block):
        span = pl.ds(row, height)
        acc_ref[tile, span] = acc_ref[tile, span] + block.astype(jnp.float32)

    def received(b, slot):
        crosses, tile, row = unpack(partner_ref[b])

        @pl.when(crosses == 1)
        def _():
            add(tile, row, got_ref[slot])

        return slot + crosses

    lax.fori_loop(0, count, received, jnp.int32(0))
    fetch.wait()

    def own(b, _):
        crosses, tile, row = unpack(code_ref[b])

        @pl.when(crosses == 0)
        def _():
            add(tile, row, own_ref[b])

        return 0

    lax.fori_loop(0, count, own, 0)

    strips = rows // SUBLANES

    def dense(tile, part):
        return jnp.concatenate(
            [
                flat[tile, pl.ds(k * parts + part, SUBLANES, stride=strips * parts)]
                for k in range(strips)
            ],
            axis=0,
        )

    def hand_over(i, _):
        for part in range(parts):
            near_ref[i, part] = dense(4 * i + 1, part).astype(near_ref.dtype)
            far_ref[i, part] = dense(4 * i + 3, part).astype(far_ref.dtype)
            keep_ref[2 * i, part] = dense(4 * i, part)
            keep_ref[2 * i + 1, part] = dense(4 * i + 2, part)
        return 0

    lax.fori_loop(0, tiles // 4, hand_over, 0)


def deposit(codes, partner_codes, view, got, date, tiles, token):
    blocks, height, _, parts, lanes = view.shape
    half = (tiles // 4, parts, TR, lanes)
    return pl.pallas_call(
        functools.partial(deposit_kernel, date),
        in_specs=[SMEM, SMEM, ANY, VMEM, ANY],
        out_specs=[VMEM, VMEM, VMEM],
        out_shape=[
            jax.ShapeDtypeStruct(half, view.dtype),
            jax.ShapeDtypeStruct(half, view.dtype),
            jax.ShapeDtypeStruct((tiles // 2,) + half[1:], jnp.float32),
        ],
        scratch_shapes=[
            pltpu.VMEM((tiles, TR, parts, lanes), jnp.float32),
            pltpu.VMEM((blocks, height, parts, lanes), view.dtype),
            pltpu.SemaphoreType.DMA,
        ],
        cost_estimate=CHEAP,
        compiler_params=params(DEPOSIT_MIB),
        name="deposit",
    )(codes, partner_codes, view, got, token)


def merge_kernel(places, *refs):
    *addend_refs, token_ref, out_ref = refs
    del token_ref
    for k, row in enumerate(zip(*places)):
        total = sum(ref[place].astype(jnp.float32) for ref, place in zip(addend_refs, row))
        out_ref[k] = total.astype(out_ref.dtype)


def merge(addends, dtype, token):
    arrays = [array for array, _ in addends]
    places = [tuple(place) for _, place in addends]
    return pl.pallas_call(
        functools.partial(merge_kernel, places),
        in_specs=[VMEM] * len(arrays) + [ANY],
        out_specs=VMEM,
        out_shape=jax.ShapeDtypeStruct((len(places[0]),) + arrays[0].shape[1:], dtype),
        cost_estimate=CHEAP,
        compiler_params=params(DEPOSIT_MIB),
        name="merge",
    )(*arrays, token)


def split(value):
    high = value.astype(jnp.bfloat16)
    return high, (value - high.astype(jnp.float32)).astype(jnp.bfloat16)


def band(size, reach):
    row = lax.broadcasted_iota(jnp.int32, (size, size), 0)
    col = lax.broadcasted_iota(jnp.int32, (size, size), 1)
    return (jnp.abs(row - col) <= reach).astype(jnp.bfloat16)


def shifted(strip, by):
    row = lax.broadcasted_iota(jnp.int32, strip.shape, 0)
    edge = 0 if by > 0 else SUBLANES - 1
    return jnp.where(row == edge, 0.0, pltpu.roll(strip, by % SUBLANES, axis=0))


def boxes(cols):
    col_band = band(cols, 7)

    def box(value):
        strips = [value[k : k + SUBLANES] for k in range(0, value.shape[0], SUBLANES)]
        strips = [shifted(s, 1) for s in strips[-3:]] + strips + [shifted(s, -1) for s in strips[:3]]
        two = [a + b for a, b in zip(strips, strips[1:])]
        four = [a + b for a, b in zip(two, two[2:])]
        seven = [a + b + c for a, b, c in zip(four, two[4:], strips[6:])]
        high, low = split(jnp.concatenate(seven, axis=0))
        wide = jnp.dot(high, col_band, preferred_element_type=jnp.float32)
        return wide + jnp.dot(low, col_band, preferred_element_type=jnp.float32)

    return box


def component(ref, part, halves):
    sides = [ref[2 * half + part] for half in range(halves)]
    return jnp.concatenate(sides, axis=-1).astype(jnp.float32)


def coherence_kernel(pairs_ref, *refs):
    *field_refs, out_ref, stack, done, sems = refs
    rows, pairs, cols = out_ref.shape
    halves = cols // LANES
    strips = rows // SUBLANES
    box = boxes(cols)
    for k, ref in enumerate(field_refs):
        stack[k] = ref[...]
    for p in range(pairs):
        u, v = stack.at[pairs_ref[2 * p]], stack.at[pairs_ref[2 * p + 1]]
        u0, u1 = component(u, 0, halves), component(u, 1, halves)
        v0, v1 = component(v, 0, halves), component(v, 1, halves)
        box_re = box(u0 * v0 + u1 * v1)
        box_im = box(u1 * v0 - u0 * v1)
        box_a = box(u0 * u0 + u1 * u1)
        box_e = box(v0 * v0 + v1 * v1)
        value = jnp.sqrt(box_re * box_re + box_im * box_im) * lax.rsqrt(
            jnp.maximum(box_a * box_e, 1.0)
        )
        for half in range(halves):
            side = done.at[half].reshape(rows * pairs, LANES)
            for k in range(strips):
                place = pl.ds(p + pairs * k, SUBLANES, stride=pairs * strips)
                side[place] = value[k * SUBLANES : (k + 1) * SUBLANES, half * LANES : (half + 1) * LANES]
    leaving = [
        pltpu.make_async_copy(done.at[half], out_ref.at[:, :, pl.ds(half * LANES, LANES)], sems.at[half])
        for half in range(halves)
    ]
    for copy in leaving:
        copy.start()
    for copy in leaving:
        copy.wait()


def coherence(pairs, fields, out_shape):
    rows, pair_count, cols = out_shape
    return pl.pallas_call(
        coherence_kernel,
        in_specs=[SMEM] + [VMEM] * len(fields),
        out_specs=ANY,
        out_shape=jax.ShapeDtypeStruct(out_shape, jnp.float32),
        scratch_shapes=[
            pltpu.VMEM((len(fields),) + fields[0].shape, fields[0].dtype),
            pltpu.VMEM((cols // LANES, rows, pair_count, LANES), jnp.float32),
            pltpu.SemaphoreType.DMA((cols // LANES,)),
        ],
        compiler_params=params(DEPOSIT_MIB),
        name="coherence",
    )(pairs, *fields)


def chunk_plan(dates, bits):
    straight = tuple(range(bits))
    return [(0, straight[1:2] + straight[:1] + straight[2:])] + [(date, straight) for date in range(1, dates)]


PICK_MIB = 60
PICK_STEPS = 4
DEPOSIT_MIB = 48
ORDER = (1, 0, 2, 1, 3, 1, 0, 2, 1, 2, 3, 2, 0, 3, 0, 3)


def local(radar_echoes, destination_panel, panel_line_shift, epoch_couples):
    blocks, height, dates_here, components, cols = radar_echoes.shape
    tile_count = lax.axis_size("tile")
    group_count = lax.axis_size("date")
    here = lax.axis_index("tile")
    group = lax.axis_index("date")
    capacity = max(2, blocks // tile_count + max(1, blocks // (2 * tile_count)))
    slots = min(blocks, tile_count // 2 * capacity)
    bits = tile_count.bit_length() - 1
    stages = bits + 1

    halves = cols // LANES
    view = radar_echoes.reshape(blocks, height, dates_here, components, halves, LANES)
    view = view.transpose(0, 1, 2, 4, 3, 5)
    view = view.reshape(blocks, height, dates_here, halves * components, LANES)

    chunks = chunk_plan(dates_here, bits)
    codes = {}
    partner_codes = {}
    for _, bit_order in chunks:
        if bit_order not in codes:
            codes[bit_order] = block_codes(destination_panel[:, 0], panel_line_shift, here, bit_order)
            partner_codes[bit_order] = swap(codes[bit_order], "tile", 1 << bit_order[0])

    order = ORDER
    if len(order) != len(chunks) * stages:
        order = [c for _, c in sorted((2 * k + c, c) for c in range(len(chunks)) for k in range(stages))]
    state = [None] * len(chunks)
    step = [0] * len(chunks)
    fields = [None] * (group_count * dates_here)
    tokens = list(partner_codes.values())
    for c in order:
        date, bit_order = chunks[c]
        k = step[c]
        step[c] += 1
        flip = [lambda value, bit=bit: swap(value, "tile", 1 << bit) for bit in bit_order]
        if k == 0:
            token = pick(codes[bit_order], view, date, slots, tokens)
            tokens = [token]
            state[c] = flip[0](token)
            continue
        if k == 1:
            far, near, keep = deposit(
                codes[bit_order], partner_codes[bit_order], view, state[c], date, tile_count // 2, token
            )
            token = far
            state[c] = [(keep, range(keep.shape[0]))], flip[1](near), flip[1](far)
            continue
        addends, near, far = state[c]
        if k < bits:
            onward = [(array, places[1::2]) for array, places in addends]
            sent = merge(onward + [(far, range(far.shape[0]))], view.dtype, token)
            token = sent
            addends = [(array, places[0::2]) for array, places in addends]
            addends = addends + [(near, range(near.shape[0]))]
            if sent.shape[0] == 1:
                state[c] = addends, None, flip[k](sent)
            else:
                state[c] = addends, flip[k](sent[0::2]), flip[k](sent[1::2])
            continue
        token = merge(addends + [(far, range(1))], view.dtype, token)
        known = {0: token[0]}
        mask = group_count // 2
        while mask:
            known.update({g ^ mask: swap(f, "date", mask) for g, f in list(known.items())})
            mask //= 2
        for g, f in known.items():
            fields[g * dates_here + date] = f

    pairs_here = epoch_couples.shape[0] // group_count
    mine = lax.dynamic_slice_in_dim(epoch_couples, group * pairs_here, pairs_here, axis=0)
    place = jnp.bitwise_xor(mine // dates_here, group) * dates_here + mine % dates_here
    return coherence(place.reshape(-1), fields, (TR, pairs_here, cols))


def solution(mesh):
    in_specs = (P("tile", None, "date", None, None), P("tile", None), P("tile"), P())
    out_specs = P("tile", "date", None)
    return jax.shard_map(local, mesh=mesh, in_specs=in_specs, out_specs=out_specs, check_vma=False)
```

```python
import functools

import jax
import jax.numpy as jnp
from jax import lax
from jax.experimental import pallas as pl
from jax.experimental.pallas import tpu as pltpu
from jax.sharding import PartitionSpec as P

TR = 256
LANES = 128
SUBLANES = 8
MIB = 1024 * 1024
CHEAP = pl.CostEstimate(flops=1, bytes_accessed=1, transcendentals=0)
SMEM = pl.BlockSpec(memory_space=pltpu.SMEM)
VMEM = pl.BlockSpec(memory_space=pltpu.VMEM)
ANY = pl.BlockSpec(memory_space=pl.ANY)


def params(mib):
    return pltpu.CompilerParams(vmem_limit_bytes=mib * MIB)


def swap(value, axis, mask):
    pairs = [(i, i ^ mask) for i in range(lax.axis_size(axis))]
    return lax.ppermute(value, axis, pairs)


def placed(target, here, order):
    relative = jnp.bitwise_xor(target, here)
    first, *others = [
        jnp.bitwise_and(lax.shift_right_logical(relative, bit), 1) for bit in order
    ]
    return first, sum(bit * (1 << k) for k, bit in enumerate(others))


def pick_kernel(order, target_ref, table_ref, blocks_ref, *refs):
    out_ref = refs[-1]
    here = lax.axis_index("tile")

    def body(b, count):
        crosses, _ = placed(target_ref[b], here, order)

        @pl.when(crosses == 1)
        def _():
            out_ref[count] = blocks_ref[b, :, 0]

        return count + crosses

    lax.fori_loop(0, blocks_ref.shape[0], body, jnp.int32(0))
    blocks = table_ref.shape[1]
    last = out_ref.shape[0] - 1
    parts, lanes = out_ref.shape[2:]
    table = jnp.zeros((parts, lanes), jnp.float32)
    wide = jnp.concatenate(
        [table_ref[...].astype(jnp.float32), jnp.zeros((2, lanes - blocks), jnp.float32)], axis=1
    )
    row = lax.broadcasted_iota(jnp.int32, (parts, lanes), 0)
    for k in range(2):
        table = jnp.where(row == k, wide[k : k + 1], table)
    out_ref[last, 0] = table.astype(out_ref.dtype)


def pick(targets, table, view, chunk, slots, tokens):
    date, order = chunk
    blocks, height, _, parts, lanes = view.shape
    return pl.pallas_call(
        functools.partial(pick_kernel, order),
        grid=(1,),
        in_specs=[
            SMEM,
            VMEM,
            pl.BlockSpec((blocks, height, 1, parts, lanes), lambda i: (0, 0, date, 0, 0)),
        ]
        + [ANY] * len(tokens),
        out_specs=VMEM,
        out_shape=jax.ShapeDtypeStruct((slots + 1, height, parts, lanes), view.dtype),
        cost_estimate=CHEAP,
        compiler_params=params(PICK_MIB),
        name="pick",
    )(targets, table, view, *tokens)


def own_kernel(date, order, target_ref, row_ref, view_ref, token_ref, acc_ref, own_ref, sem):
    del token_ref
    count, height = own_ref.shape[:2]
    tiles, rows, parts, lanes = acc_ref.shape
    here = lax.axis_index("tile")
    fetch = pltpu.make_async_copy(view_ref.at[:, :, date], own_ref, sem)
    fetch.start()
    flat = acc_ref.reshape(tiles, rows * parts, lanes)

    def clear(t, _):
        flat[t] = jnp.zeros((rows * parts, lanes), jnp.float32)
        return 0

    lax.fori_loop(0, tiles, clear, 0)
    fetch.wait()

    def own(b, _):
        crosses, tile = placed(target_ref[b], here, order)

        @pl.when(crosses == 0)
        def _():
            span = pl.ds(row_ref[b], height)
            acc_ref[tile, span] = acc_ref[tile, span] + own_ref[b].astype(jnp.float32)

        return 0

    lax.fori_loop(0, count, own, 0)


def own_sums(targets, first_rows, view, chunk, tiles, token):
    date, order = chunk
    blocks, height, _, parts, lanes = view.shape
    return pl.pallas_call(
        functools.partial(own_kernel, date, order),
        in_specs=[SMEM, SMEM, ANY, ANY],
        out_specs=VMEM,
        out_shape=jax.ShapeDtypeStruct((tiles, TR, parts, lanes), jnp.float32),
        scratch_shapes=[
            pltpu.VMEM((blocks, height, parts, lanes), view.dtype),
            pltpu.SemaphoreType.DMA,
        ],
        cost_estimate=CHEAP,
        compiler_params=params(DEPOSIT_MIB),
        name="own",
    )(targets, first_rows, view, token)


def deposit_kernel(
    order, count, sums_ref, got_ref, token_ref, far_ref, near_ref, keep_ref, acc_ref, table_ref, code_ref, sem
):
    del token_ref
    height = got_ref.shape[1]
    tiles, rows, parts, lanes = acc_ref.shape
    here = lax.axis_index("tile")
    table = got_ref[got_ref.shape[0] - 1, 0].astype(jnp.float32).astype(jnp.int32)
    table_ref[0:2] = table[0:2]
    inform = pltpu.make_async_copy(table_ref, code_ref, sem)
    inform.start()
    flat = acc_ref.reshape(tiles, rows * parts, lanes)
    flat_sums = sums_ref.reshape(tiles, rows * parts, lanes)

    def begin(t, _):
        flat[t] = flat_sums[t]
        return 0

    lax.fori_loop(0, tiles, begin, 0)
    inform.wait()

    def received(b, slot):
        away, tile = placed(code_ref[0, b], here, order)

        @pl.when(away == 0)
        def _():
            span = pl.ds(code_ref[1, b], height)
            acc_ref[tile, span] = acc_ref[tile, span] + got_ref[slot].astype(jnp.float32)

        return slot + 1 - away

    lax.fori_loop(0, count, received, jnp.int32(0))
    strips = rows // SUBLANES

    def dense(tile, part):
        return jnp.concatenate(
            [
                flat[tile, pl.ds(k * parts + part, SUBLANES, stride=strips * parts)]
                for k in range(strips)
            ],
            axis=0,
        )

    def hand_over(i, _):
        for part in range(parts):
            near_ref[i, part] = dense(4 * i + 1, part).astype(near_ref.dtype)
            far_ref[i, part] = dense(4 * i + 3, part).astype(far_ref.dtype)
            keep_ref[2 * i, part] = dense(4 * i, part)
            keep_ref[2 * i + 1, part] = dense(4 * i + 2, part)
        return 0

    lax.fori_loop(0, tiles // 4, hand_over, 0)


def deposit(sums, got, chunk, blocks, token):
    _, order = chunk
    tiles, rows, parts, lanes = sums.shape
    half = (tiles // 4, parts, rows, lanes)
    return pl.pallas_call(
        functools.partial(deposit_kernel, order, blocks),
        in_specs=[VMEM, VMEM, ANY],
        out_specs=[VMEM, VMEM, VMEM],
        out_shape=[
            jax.ShapeDtypeStruct(half, got.dtype),
            jax.ShapeDtypeStruct(half, got.dtype),
            jax.ShapeDtypeStruct((tiles // 2,) + half[1:], jnp.float32),
        ],
        scratch_shapes=[
            pltpu.VMEM(sums.shape, jnp.float32),
            pltpu.VMEM((SUBLANES, lanes), jnp.int32),
            pltpu.SMEM((SUBLANES, lanes), jnp.int32),
            pltpu.SemaphoreType.DMA,
        ],
        cost_estimate=CHEAP,
        compiler_params=params(DEPOSIT_MIB),
        name="deposit",
    )(sums, got, token)


def merge_kernel(places, *refs):
    *addend_refs, token_ref, out_ref = refs
    del token_ref
    for k, row in enumerate(zip(*places)):
        total = sum(ref[place].astype(jnp.float32) for ref, place in zip(addend_refs, row))
        out_ref[k] = total.astype(out_ref.dtype)


def merge(addends, dtype, token):
    arrays = [array for array, _ in addends]
    places = [tuple(place) for _, place in addends]
    return pl.pallas_call(
        functools.partial(merge_kernel, places),
        in_specs=[VMEM] * len(arrays) + [SMEM if token.ndim == 1 else ANY],
        out_specs=VMEM,
        out_shape=jax.ShapeDtypeStruct((len(places[0]),) + arrays[0].shape[1:], dtype),
        cost_estimate=CHEAP,
        compiler_params=params(DEPOSIT_MIB),
        name="merge",
    )(*arrays, token)


def split(value):
    high = value.astype(jnp.bfloat16)
    return high, (value - high.astype(jnp.float32)).astype(jnp.bfloat16)


def band(size, reach):
    row = lax.broadcasted_iota(jnp.int32, (size, size), 0)
    col = lax.broadcasted_iota(jnp.int32, (size, size), 1)
    return (jnp.abs(row - col) <= reach).astype(jnp.bfloat16)


def shifted(strip, by):
    row = lax.broadcasted_iota(jnp.int32, strip.shape, 0)
    edge = 0 if by > 0 else SUBLANES - 1
    return jnp.where(row == edge, 0.0, pltpu.roll(strip, by % SUBLANES, axis=0))


def boxes(cols):
    col_band = band(cols, 7)

    def box(value):
        strips = [value[k : k + SUBLANES] for k in range(0, value.shape[0], SUBLANES)]
        strips = [shifted(s, 1) for s in strips[-3:]] + strips + [shifted(s, -1) for s in strips[:3]]
        two = [a + b for a, b in zip(strips, strips[1:])]
        four = [a + b for a, b in zip(two, two[2:])]
        seven = [a + b + c for a, b, c in zip(four, two[4:], strips[6:])]
        high, low = split(jnp.concatenate(seven, axis=0))
        wide = jnp.dot(high, col_band, preferred_element_type=jnp.float32)
        return wide + jnp.dot(low, col_band, preferred_element_type=jnp.float32)

    return box


def component(ref, part, halves):
    sides = [ref[2 * half + part] for half in range(halves)]
    return jnp.concatenate(sides, axis=-1).astype(jnp.float32)


def power_box(box, ref, cols):
    halves = cols // LANES
    u0, u1 = component(ref, 0, halves), component(ref, 1, halves)
    return box(u0 * u0 + u1 * u1)


def early_kernel(*refs):
    *field_refs, token_ref, stack_ref, power_ref, end_ref = refs
    del token_ref
    end_ref[0] = 0
    cols = power_ref.shape[2]
    box = boxes(cols)
    for k, ref in enumerate(field_refs):
        stack_ref[k] = ref[...]
        power_ref[k] = power_box(box, ref, cols)


def collect(fields, rows, cols, token):
    return pl.pallas_call(
        early_kernel,
        in_specs=[VMEM] * len(fields) + [ANY],
        out_specs=[VMEM, VMEM, SMEM],
        out_shape=[
            jax.ShapeDtypeStruct((len(fields),) + fields[0].shape, fields[0].dtype),
            jax.ShapeDtypeStruct((len(fields), rows, cols), jnp.float32),
            jax.ShapeDtypeStruct((1,), jnp.int32),
        ],
        cost_estimate=CHEAP,
        compiler_params=params(DEPOSIT_MIB),
        name="collect",
    )(*fields, token)


def coherence_kernel(pairs_ref, *refs):
    *field_refs, stack_ref, power_ref, out_ref, stack, power, done, sems = refs
    rows, pairs, cols = out_ref.shape
    halves = cols // LANES
    strips = rows // SUBLANES
    box = boxes(cols)
    early = stack_ref.shape[0]
    for k in range(early):
        stack[k] = stack_ref[k]
        power[k] = power_ref[k]
    for k, ref in enumerate(field_refs):
        stack[early + k] = ref[...]
        power[early + k] = power_box(box, ref, cols)
    for p in range(pairs):
        first, second = pairs_ref[2 * p], pairs_ref[2 * p + 1]
        u, v = stack.at[first], stack.at[second]
        u0, u1 = component(u, 0, halves), component(u, 1, halves)
        v0, v1 = component(v, 0, halves), component(v, 1, halves)
        box_re = box(u0 * v0 + u1 * v1)
        box_im = box(u1 * v0 - u0 * v1)
        value = jnp.sqrt(box_re * box_re + box_im * box_im) * lax.rsqrt(
            jnp.maximum(power[first] * power[second], 1.0)
        )
        for half in range(halves):
            side = done.at[half].reshape(rows * pairs, LANES)
            for k in range(strips):
                place = pl.ds(p + pairs * k, SUBLANES, stride=pairs * strips)
                side[place] = value[k * SUBLANES : (k + 1) * SUBLANES, half * LANES : (half + 1) * LANES]
    leaving = [
        pltpu.make_async_copy(done.at[half], out_ref.at[:, :, pl.ds(half * LANES, LANES)], sems.at[half])
        for half in range(halves)
    ]
    for copy in leaving:
        copy.start()
    for copy in leaving:
        copy.wait()


def coherence(pairs, fields, stack, power, out_shape):
    rows, pair_count, cols = out_shape
    total = len(fields) + stack.shape[0]
    return pl.pallas_call(
        coherence_kernel,
        in_specs=[SMEM] + [VMEM] * (len(fields) + 2),
        out_specs=ANY,
        out_shape=jax.ShapeDtypeStruct(out_shape, jnp.float32),
        scratch_shapes=[
            pltpu.VMEM((total,) + fields[0].shape, fields[0].dtype),
            pltpu.VMEM((total, rows, cols), jnp.float32),
            pltpu.VMEM((cols // LANES, rows, pair_count, LANES), jnp.float32),
            pltpu.SemaphoreType.DMA((cols // LANES,)),
        ],
        compiler_params=params(LAST_MIB),
        name="coherence",
    )(pairs, *fields, stack, power)


def chunk_plan(dates, bits):
    straight = tuple(range(bits))
    crossed = straight[1:2] + straight[:1] + straight[2:]
    return [(date, crossed if date < CROSSED else straight) for date in range(dates)]


CROSSED = 1
PICK_MIB = 60
DEPOSIT_MIB = 16
LAST_MIB = 32
ORDER = (1, 0, 2, 3, 1, 0, 1, 0, 2, 1, 2, 1, 2, 3, 3, 0, 2, 3, 0, 3)


def local(radar_echoes, destination_panel, panel_line_shift, epoch_couples):
    blocks, height, dates_here, components, cols = radar_echoes.shape
    tile_count = lax.axis_size("tile")
    group_count = lax.axis_size("date")
    group = lax.axis_index("date")
    capacity = max(2, blocks // tile_count + max(1, blocks // (2 * tile_count)))
    slots = min(blocks, tile_count // 2 * capacity)
    bits = tile_count.bit_length() - 1
    stages = bits + 2

    halves = cols // LANES
    view = radar_echoes.reshape(blocks, height, dates_here, components, halves, LANES)
    view = view.transpose(0, 1, 2, 4, 3, 5)
    view = view.reshape(blocks, height, dates_here, halves * components, LANES)

    chunks = chunk_plan(dates_here, bits)
    targets = destination_panel[:, 0]
    table = jnp.stack([targets, panel_line_shift])
    order = ORDER
    if len(order) != len(chunks) * stages:
        order = [c for _, c in sorted((2 * k + c, c) for c in range(len(chunks)) for k in range(stages))]
    state = [None] * len(chunks)
    step = [0] * len(chunks)
    fields = [None] * dates_here
    finished = []
    tokens = []
    for c in order:
        date, bit_order = chunks[c]
        k = step[c]
        step[c] += 1
        flip = [lambda value, bit=bit: swap(value, "tile", 1 << bit) for bit in bit_order]
        if k == 0:
            token = pick(targets, table, view, chunks[c], slots, tokens)
            tokens = [token]
            state[c] = flip[0](token)
            continue
        if k == 1:
            token = own_sums(targets, panel_line_shift, view, chunks[c], tile_count // 2, token)
            state[c] = token, state[c]
            continue
        k -= 1
        if k == 1:
            far, near, keep = deposit(*state[c], chunks[c], blocks, token)
            token = far
            state[c] = [(keep, range(keep.shape[0]))], flip[1](near), flip[1](far)
            continue
        addends, near, far = state[c]
        if k < bits:
            onward = [(array, places[1::2]) for array, places in addends]
            sent = merge(onward + [(far, range(far.shape[0]))], view.dtype, token)
            token = sent
            addends = [(array, places[0::2]) for array, places in addends]
            addends = addends + [(near, range(near.shape[0]))]
            if sent.shape[0] == 1:
                state[c] = addends, None, flip[k](sent)
            else:
                state[c] = addends, flip[k](sent[0::2]), flip[k](sent[1::2])
            continue
        if len(finished) == len(chunks) - 1:
            held = [fields[chunks[e][0]][g] for e in finished[:-1] for g in range(group_count)]
            stack, power, token = collect(held, TR, cols, token)
        finished.append(c)
        token = merge(addends + [(far, range(1))], view.dtype, token)
        known = {0: token[0]}
        mask = group_count // 2
        while mask:
            known.update({g ^ mask: swap(f, "date", mask) for g, f in list(known.items())})
            mask //= 2
        fields[date] = known

    late = [fields[chunks[e][0]][g] for e in finished[-2:] for g in range(group_count)]
    slot_of = [0] * dates_here
    for k, e in enumerate(finished):
        slot_of[chunks[e][0]] = k * group_count
    pairs_here = epoch_couples.shape[0] // group_count
    mine = lax.dynamic_slice_in_dim(epoch_couples, group * pairs_here, pairs_here, axis=0)
    date = mine % dates_here
    slot = sum([jnp.where(date == k, first, 0) for k, first in enumerate(slot_of)], jnp.zeros_like(date))
    place = slot + jnp.bitwise_xor(mine // dates_here, group)
    return coherence(place.reshape(-1), late, stack, power, (TR, pairs_here, cols))


def solution(mesh):
    in_specs = (P("tile", None, "date", None, None), P("tile", None), P("tile"), P())
    out_specs = P("tile", "date", None)
    return jax.shard_map(local, mesh=mesh, in_specs=in_specs, out_specs=out_specs, check_vma=False)
```

```python
import functools

import jax
import jax.numpy as jnp
from jax import lax
from jax.experimental import pallas as pl
from jax.experimental.pallas import tpu as pltpu
from jax.sharding import PartitionSpec as P

TR = 256
LANES = 128
SUBLANES = 8
MIB = 1024 * 1024
CHEAP = pl.CostEstimate(flops=1, bytes_accessed=1, transcendentals=0)
SMEM = pl.BlockSpec(memory_space=pltpu.SMEM)
VMEM = pl.BlockSpec(memory_space=pltpu.VMEM)
ANY = pl.BlockSpec(memory_space=pl.ANY)


def params(mib):
    return pltpu.CompilerParams(vmem_limit_bytes=mib * MIB)


def swap(value, axis, mask):
    pairs = [(i, i ^ mask) for i in range(lax.axis_size(axis))]
    return lax.ppermute(value, axis, pairs)


def placed(target, here, order):
    relative = jnp.bitwise_xor(target, here)
    first, *others = [
        jnp.bitwise_and(lax.shift_right_logical(relative, bit), 1) for bit in order
    ]
    return first, sum(bit * (1 << k) for k, bit in enumerate(others))


def pick_kernel(order, target_ref, targets_ref, rows_ref, blocks_ref, *refs):
    out_ref = refs[-1]
    here = lax.axis_index("tile")

    def body(b, count):
        crosses, _ = placed(target_ref[b], here, order)

        @pl.when(crosses == 1)
        def _():
            out_ref[count] = blocks_ref[b, :, 0]

        return count + crosses

    lax.fori_loop(0, blocks_ref.shape[0], body, jnp.int32(0))
    blocks = targets_ref.shape[1]
    last = out_ref.shape[0] - 1
    parts, lanes = out_ref.shape[2:]
    table = jnp.zeros((parts, lanes), jnp.float32)
    row = lax.broadcasted_iota(jnp.int32, (parts, lanes), 0)
    for k, ref in enumerate((targets_ref, rows_ref)):
        line = ref[...].astype(jnp.float32)
        if lanes > blocks:
            line = jnp.concatenate([line, jnp.zeros((1, lanes - blocks), jnp.float32)], axis=1)
        table = jnp.where(row == k, line, table)
    out_ref[last, 0] = table.astype(out_ref.dtype)


def pick(targets, first_rows, view, chunk, slots, tokens):
    date, order = chunk
    blocks, height, _, parts, lanes = view.shape
    return pl.pallas_call(
        functools.partial(pick_kernel, order),
        grid=(1,),
        in_specs=[
            SMEM,
            pl.BlockSpec((1, blocks), lambda i: (0, 0)),
            pl.BlockSpec((1, blocks), lambda i: (0, 0)),
            pl.BlockSpec((blocks, height, 1, parts, lanes), lambda i: (0, 0, date, 0, 0)),
        ]
        + [ANY] * len(tokens),
        out_specs=VMEM,
        out_shape=jax.ShapeDtypeStruct((slots + 1, height, parts, lanes), view.dtype),
        cost_estimate=CHEAP,
        compiler_params=params(PICK_MIB),
        name="pick",
    )(targets, targets.reshape(1, blocks), first_rows.reshape(1, blocks), view, *tokens)


def own_kernel(date, order, target_ref, row_ref, view_ref, token_ref, acc_ref, own_ref, sem):
    del token_ref
    count, height = own_ref.shape[:2]
    tiles, rows, parts, lanes = acc_ref.shape
    here = lax.axis_index("tile")
    fetch = pltpu.make_async_copy(view_ref.at[:, :, date], own_ref, sem)
    fetch.start()
    flat = acc_ref.reshape(tiles, rows * parts, lanes)

    def clear(t, _):
        flat[t] = jnp.zeros((rows * parts, lanes), jnp.float32)
        return 0

    lax.fori_loop(0, tiles, clear, 0)
    fetch.wait()

    def own(b, _):
        crosses, tile = placed(target_ref[b], here, order)

        @pl.when(crosses == 0)
        def _():
            span = pl.ds(row_ref[b], height)
            acc_ref[tile, span] = acc_ref[tile, span] + own_ref[b].astype(jnp.float32)

        return 0

    lax.fori_loop(0, count, own, 0)


def own_sums(targets, first_rows, view, chunk, tiles, token):
    date, order = chunk
    blocks, height, _, parts, lanes = view.shape
    return pl.pallas_call(
        functools.partial(own_kernel, date, order),
        in_specs=[SMEM, SMEM, ANY, ANY],
        out_specs=VMEM,
        out_shape=jax.ShapeDtypeStruct((tiles, TR, parts, lanes), jnp.float32),
        scratch_shapes=[
            pltpu.VMEM((blocks, height, parts, lanes), view.dtype),
            pltpu.SemaphoreType.DMA,
        ],
        cost_estimate=CHEAP,
        compiler_params=params(DEPOSIT_MIB),
        name="own",
    )(targets, first_rows, view, token)


def deposit_kernel(
    order, count, sums_ref, got_ref, token_ref, far_ref, near_ref, keep_ref, acc_ref, table_ref, code_ref, sem
):
    del token_ref
    height = got_ref.shape[1]
    tiles, rows, parts, lanes = acc_ref.shape
    here = lax.axis_index("tile")
    table = got_ref[got_ref.shape[0] - 1, 0].astype(jnp.float32).astype(jnp.int32)
    table_ref[0:2] = table[0:2]
    inform = pltpu.make_async_copy(table_ref, code_ref, sem)
    inform.start()
    flat = acc_ref.reshape(tiles, rows * parts, lanes)
    flat_sums = sums_ref.reshape(tiles, rows * parts, lanes)

    def begin(t, _):
        flat[t] = flat_sums[t]
        return 0

    lax.fori_loop(0, tiles, begin, 0)
    inform.wait()

    def received(b, slot):
        away, tile = placed(code_ref[0, b], here, order)

        @pl.when(away == 0)
        def _():
            span = pl.ds(code_ref[1, b], height)
            acc_ref[tile, span] = acc_ref[tile, span] + got_ref[slot].astype(jnp.float32)

        return slot + 1 - away

    lax.fori_loop(0, count, received, jnp.int32(0))
    strips = rows // SUBLANES

    def dense(tile, part):
        return jnp.concatenate(
            [
                flat[tile, pl.ds(k * parts + part, SUBLANES, stride=strips * parts)]
                for k in range(strips)
            ],
            axis=0,
        )

    def hand_over(i, _):
        for part in range(parts):
            near_ref[i, part] = dense(4 * i + 1, part).astype(near_ref.dtype)
            far_ref[i, part] = dense(4 * i + 3, part).astype(far_ref.dtype)
            keep_ref[2 * i, part] = dense(4 * i, part)
            keep_ref[2 * i + 1, part] = dense(4 * i + 2, part)
        return 0

    lax.fori_loop(0, tiles // 4, hand_over, 0)


def deposit(sums, got, chunk, blocks, token):
    _, order = chunk
    tiles, rows, parts, lanes = sums.shape
    half = (tiles // 4, parts, rows, lanes)
    return pl.pallas_call(
        functools.partial(deposit_kernel, order, blocks),
        in_specs=[VMEM, VMEM, ANY],
        out_specs=[VMEM, VMEM, VMEM],
        out_shape=[
            jax.ShapeDtypeStruct(half, got.dtype),
            jax.ShapeDtypeStruct(half, got.dtype),
            jax.ShapeDtypeStruct((tiles // 2,) + half[1:], jnp.float32),
        ],
        scratch_shapes=[
            pltpu.VMEM(sums.shape, jnp.float32),
            pltpu.VMEM((SUBLANES, lanes), jnp.int32),
            pltpu.SMEM((SUBLANES, lanes), jnp.int32),
            pltpu.SemaphoreType.DMA,
        ],
        cost_estimate=CHEAP,
        compiler_params=params(DEPOSIT_MIB),
        name="deposit",
    )(sums, got, token)


def merge_kernel(places, *refs):
    *addend_refs, token_ref, out_ref = refs
    del token_ref
    for k, row in enumerate(zip(*places)):
        total = sum(ref[place].astype(jnp.float32) for ref, place in zip(addend_refs, row))
        out_ref[k] = total.astype(out_ref.dtype)


def merge(addends, dtype, token):
    arrays = [array for array, _ in addends]
    places = [tuple(place) for _, place in addends]
    return pl.pallas_call(
        functools.partial(merge_kernel, places),
        in_specs=[VMEM] * len(arrays) + [SMEM if token.ndim == 1 else ANY],
        out_specs=VMEM,
        out_shape=jax.ShapeDtypeStruct((len(places[0]),) + arrays[0].shape[1:], dtype),
        cost_estimate=CHEAP,
        compiler_params=params(DEPOSIT_MIB),
        name="merge",
    )(*arrays, token)


def split(value):
    high = value.astype(jnp.bfloat16)
    return high, (value - high.astype(jnp.float32)).astype(jnp.bfloat16)


def band(size, reach):
    row = lax.broadcasted_iota(jnp.int32, (size, size), 0)
    col = lax.broadcasted_iota(jnp.int32, (size, size), 1)
    return (jnp.abs(row - col) <= reach).astype(jnp.bfloat16)


def shifted(strip, by):
    row = lax.broadcasted_iota(jnp.int32, strip.shape, 0)
    edge = 0 if by > 0 else SUBLANES - 1
    return jnp.where(row == edge, 0.0, pltpu.roll(strip, by % SUBLANES, axis=0))


def boxes(cols):
    col_band = band(cols, 7)

    def box(value):
        strips = [value[k : k + SUBLANES] for k in range(0, value.shape[0], SUBLANES)]
        strips = [shifted(s, 1) for s in strips[-3:]] + strips + [shifted(s, -1) for s in strips[:3]]
        two = [a + b for a, b in zip(strips, strips[1:])]
        four = [a + b for a, b in zip(two, two[2:])]
        seven = [a + b + c for a, b, c in zip(four, two[4:], strips[6:])]
        high, low = split(jnp.concatenate(seven, axis=0))
        wide = jnp.dot(high, col_band, preferred_element_type=jnp.float32)
        return wide + jnp.dot(low, col_band, preferred_element_type=jnp.float32)

    return box


def component(ref, part, halves):
    sides = [ref[2 * half + part] for half in range(halves)]
    return jnp.concatenate(sides, axis=-1).astype(jnp.float32)


def collect_kernel(*refs):
    *field_refs, _, stack_ref, end_ref = refs
    end_ref[0] = 0
    for k, ref in enumerate(field_refs):
        stack_ref[k] = ref[...]


def collect(fields, token):
    return pl.pallas_call(
        collect_kernel,
        in_specs=[VMEM] * len(fields) + [ANY],
        out_specs=[VMEM, SMEM],
        out_shape=[
            jax.ShapeDtypeStruct((len(fields),) + fields[0].shape, fields[0].dtype),
            jax.ShapeDtypeStruct((1,), jnp.int32),
        ],
        cost_estimate=CHEAP,
        compiler_params=params(DEPOSIT_MIB),
        name="collect",
    )(*fields, token)


def coherence_kernel(pairs_ref, *refs):
    *field_refs, stack_ref, out_ref, stack, done, sems = refs
    rows, pairs, cols = out_ref.shape
    halves = cols // LANES
    strips = rows // SUBLANES
    box = boxes(cols)
    early = stack_ref.shape[0]
    for k in range(early):
        stack[k] = stack_ref[k]
    for k, ref in enumerate(field_refs):
        stack[early + k] = ref[...]
    for p in range(pairs):
        first, second = pairs_ref[2 * p], pairs_ref[2 * p + 1]
        u, v = stack.at[first], stack.at[second]
        u0, u1 = component(u, 0, halves), component(u, 1, halves)
        v0, v1 = component(v, 0, halves), component(v, 1, halves)
        box_re = box(u0 * v0 + u1 * v1)
        box_im = box(u1 * v0 - u0 * v1)
        box_a = box(u0 * u0 + u1 * u1)
        box_e = box(v0 * v0 + v1 * v1)
        value = jnp.sqrt(box_re * box_re + box_im * box_im) * lax.rsqrt(
            jnp.maximum(box_a * box_e, 1.0)
        )
        for half in range(halves):
            side = done.at[half].reshape(rows * pairs, LANES)
            for k in range(strips):
                place = pl.ds(p + pairs * k, SUBLANES, stride=pairs * strips)
                side[place] = value[k * SUBLANES : (k + 1) * SUBLANES, half * LANES : (half + 1) * LANES]
    leaving = [
        pltpu.make_async_copy(done.at[half], out_ref.at[:, :, pl.ds(half * LANES, LANES)], sems.at[half])
        for half in range(halves)
    ]
    for copy in leaving:
        copy.start()
    for copy in leaving:
        copy.wait()


def coherence(pairs, fields, stack, out_shape):
    rows, pair_count, cols = out_shape
    total = len(fields) + stack.shape[0]
    return pl.pallas_call(
        coherence_kernel,
        in_specs=[SMEM] + [VMEM] * (len(fields) + 1),
        out_specs=ANY,
        out_shape=jax.ShapeDtypeStruct(out_shape, jnp.float32),
        scratch_shapes=[
            pltpu.VMEM((total,) + fields[0].shape, fields[0].dtype),
            pltpu.VMEM((cols // LANES, rows, pair_count, LANES), jnp.float32),
            pltpu.SemaphoreType.DMA((cols // LANES,)),
        ],
        compiler_params=params(LAST_MIB),
        name="coherence",
    )(pairs, *fields, stack)


def chunk_plan(dates, bits):
    straight = tuple(range(bits))
    crossed = straight[1:2] + straight[:1] + straight[2:]
    return [(date, crossed if date < CROSSED else straight) for date in range(dates)]


CROSSED = 1
PICK_MIB = 60
DEPOSIT_MIB = 16
LAST_MIB = 32
ORDER = (1, 0, 2, 3, 1, 0, 1, 0, 2, 1, 2, 1, 2, 3, 3, 0, 2, 3, 0, 3)


def local(radar_echoes, destination_panel, panel_line_shift, epoch_couples):
    blocks, height, dates_here, components, cols = radar_echoes.shape
    tile_count = lax.axis_size("tile")
    group_count = lax.axis_size("date")
    group = lax.axis_index("date")
    capacity = max(2, blocks // tile_count + max(1, blocks // (2 * tile_count)))
    slots = min(blocks, tile_count // 2 * capacity)
    bits = tile_count.bit_length() - 1
    stages = bits + 2

    halves = cols // LANES
    view = radar_echoes.reshape(blocks, height, dates_here, components, halves, LANES)
    view = view.transpose(0, 1, 2, 4, 3, 5)
    view = view.reshape(blocks, height, dates_here, halves * components, LANES)

    chunks = chunk_plan(dates_here, bits)
    targets = destination_panel[:, 0]
    order = ORDER
    if len(order) != len(chunks) * stages:
        order = [c for _, c in sorted((2 * k + c, c) for c in range(len(chunks)) for k in range(stages))]
    slot_of = [0] * dates_here
    finishing = [c for k, c in enumerate(order) if c not in order[k + 1 :]]
    for k, c in enumerate(finishing):
        slot_of[chunks[c][0]] = k * group_count
    pairs_here = epoch_couples.shape[0] // group_count
    mine = lax.dynamic_slice_in_dim(epoch_couples, group * pairs_here, pairs_here, axis=0)
    date = mine % dates_here
    slot = sum([jnp.where(date == k, first, 0) for k, first in enumerate(slot_of)], jnp.zeros_like(date))
    place = (slot + jnp.bitwise_xor(mine // dates_here, group)).reshape(-1)
    state = [None] * len(chunks)
    step = [0] * len(chunks)
    fields = [None] * dates_here
    finished = []
    tokens = []
    for c in order:
        date, bit_order = chunks[c]
        k = step[c]
        step[c] += 1
        flip = [lambda value, bit=bit: swap(value, "tile", 1 << bit) for bit in bit_order]
        if k == 0:
            token = pick(targets, panel_line_shift, view, chunks[c], slots, tokens)
            tokens = [token]
            state[c] = flip[0](token)
            continue
        if k == 1:
            token = own_sums(targets, panel_line_shift, view, chunks[c], tile_count // 2, token)
            state[c] = token, state[c]
            continue
        k -= 1
        if k == 1:
            far, near, keep = deposit(*state[c], chunks[c], blocks, token)
            token = far
            state[c] = [(keep, range(keep.shape[0]))], flip[1](near), flip[1](far)
            continue
        addends, near, far = state[c]
        if k < bits:
            onward = [(array, places[1::2]) for array, places in addends]
            sent = merge(onward + [(far, range(far.shape[0]))], view.dtype, token)
            token = sent
            addends = [(array, places[0::2]) for array, places in addends]
            addends = addends + [(near, range(near.shape[0]))]
            if sent.shape[0] == 1:
                state[c] = addends, None, flip[k](sent)
            else:
                state[c] = addends, flip[k](sent[0::2]), flip[k](sent[1::2])
            continue
        if len(finished) == len(chunks) - 1:
            held = [fields[chunks[e][0]][g] for e in finished[:-1] for g in range(group_count)]
            stack, token = collect(held, token)
        finished.append(c)
        token = merge(addends + [(far, range(1))], view.dtype, token)
        known = {0: token[0]}
        mask = group_count // 2
        while mask:
            known.update({g ^ mask: swap(f, "date", mask) for g, f in list(known.items())})
            mask //= 2
        fields[date] = known

    late = [fields[chunks[e][0]][g] for e in finished[-2:] for g in range(group_count)]
    return coherence(place, late, stack, (TR, pairs_here, cols))


def solution(mesh):
    in_specs = (P("tile", None, "date", None, None), P("tile", None), P("tile"), P())
    out_specs = P("tile", "date", None)
    return jax.shard_map(local, mesh=mesh, in_specs=in_specs, out_specs=out_specs, check_vma=False)
```
